1024 devices in a mesh: energy: 64 (over x, y, core), slab: 16 (over z).
Axes of the slice: x: 4, y: 8, z: 16, core: 2. Of those that a mesh axis runs over, the one named last changes fastest.
Arguments:
- green_rows: float32 [2, 128, 4096, 512], P(None, 'energy', 'slab'), may hold values from -6 to 6
- less_surfaces: float32 [2, 128, 4096, 128], P(None, 'energy', 'slab'), may hold values from -6 to 6
- less_diag: float32 [2, 128, 8192], P(None, 'energy', 'slab'), may hold values from -6 to 6
- neighbours: int32 [16, 2, 8, 512], P('slab'), may hold values from 0 to 127
- hopping: float32 [16, 2, 8, 512], P('slab'), may hold values from -0.046875 to 0.046875
- damp: float32 [16, 512], P('slab'), may hold values from 0 to 1
- mode_offset: int32 [8], replicated, may hold values from 1 to 64, as said below
- mode_strength: float32 [8], replicated, may hold values from 0.002 to 0.02
- bose: float32 [8], replicated, may hold values from 0.05 to 2
Outputs:
- correction: float32 [2, 128, 4096, 128], P(None, 'energy', 'slab')
- self_energy: float32 [2, 128, 8192], P(None, 'energy', 'slab')
The draws below stay inside these ranges and needn't reach their ends.
Inputs may be any that keep to these rules, and one draw needn't show every extreme that they name: `neighbours`: a position within the facing surface of the adjacent slab. `mode_offset`: some mode has offset exactly 64.
All inputs are finite; a program needn't handle non-finite values.
Results may differ from the reference program's by a relative error of at most 0.000071.
Values sent between devices are 32-bit elements; how exact they have to be, the bound alone decides.
A program may use at most 32 MiB of HBM per device.

```python
import math
import jax
import jax.numpy as jnp
from jax import lax

SLAB_ORBITALS = 512
SURF = 128
NB = 8
MODES = 8
ENERGIES = 128
SLAB_TOTAL = 16
SPAN = 64


def draw_damp(key, part):
    rate_key, slab_key, place_key, depth_random_key = jax.random.split(jax.random.fold_in(key, 17), 4)
    low_end = 0.05
    high_end = 30.0
    decay_rate = jnp.exp(jax.random.uniform(rate_key, (1, SLAB_ORBITALS), jnp.float32, math.log(low_end), math.log(high_end)))
    factor = jnp.exp(jax.random.uniform(slab_key, (SLAB_TOTAL, SLAB_ORBITALS), jnp.float32, math.log(0.5), math.log(2.0)))
    slab_entries = jnp.exp(-decay_rate * factor / SLAB_TOTAL)
    slab_locations = jax.random.randint(place_key, (2,), 0, SLAB_TOTAL)
    slab_indices = lax.broadcasted_iota(jnp.int32, (SLAB_TOTAL, 1), 0)
    pulse_groups = jnp.any(slab_indices == slab_locations[None, :], axis=1, keepdims=True)
    pulse_depth = jax.random.uniform(depth_random_key, (SLAB_TOTAL, SLAB_ORBITALS), jnp.float32, 0.5, 0.8)
    return jnp.where(pulse_groups, slab_entries * pulse_depth, slab_entries).astype(jnp.float32)


def draw_mode_offset(key, part):
    value_key, which_key = jax.random.split(jax.random.fold_in(key, 29), 2)
    offsets = jax.random.randint(value_key, (MODES,), 1, SPAN + 1)
    chosen = jax.random.randint(which_key, (), 0, MODES)
    mode_ids = lax.broadcasted_iota(jnp.int32, (MODES,), 0)
    return jnp.where(mode_ids == chosen, SPAN, offsets).astype(jnp.int32)


def touch_ends(values, stream_key, least, largest):
    place = [jax.random.randint(jax.random.fold_in(stream_key, axis), (), 0, length) for axis, length in enumerate(values.shape)]
    widest = values.shape.index(max(values.shape))
    next_to = place[:widest] + [(place[widest] + 1) % values.shape[widest]] + place[widest + 1:]
    return values.at[tuple(place)].set(least).at[tuple(next_to)].set(largest)


def block_scale(own_key, dims, cuts, least, high):
    factor_of, own = 1.0, jax.random.fold_in(own_key, 6)
    for dim, shards_of in cuts:
        draws = jnp.exp(jax.random.uniform(jax.random.fold_in(own, dim), (shards_of,), jnp.float32, least / len(cuts), high / len(cuts)))
        factor_of = factor_of * jnp.repeat(draws, dims[dim] // shards_of).reshape([-1 if axis == dim else 1 for axis in range(len(dims))])
    return factor_of


def scatter_about(own_key, dims, width, most, cuts=(), kind=jnp.bfloat16):
    level = block_scale(own_key, dims, cuts, -0.22, 0.18) if cuts else 1.0
    array = jax.random.normal(own_key, dims, jnp.float32) * width * level
    return jnp.minimum(jnp.maximum(array, -most), most).astype(kind)


def setup_inputs(seed: int = 0) -> dict:
    key_list = jax.random.split(jax.random.key(seed), 10)
    green_rows = scatter_about(key_list[0], (2, ENERGIES, SLAB_TOTAL * 2 * SURF, SLAB_ORBITALS), 1.0, 6.0, ((1, 64), (2, 16)), jnp.float32)
    less_surfaces = scatter_about(key_list[1], (2, ENERGIES, SLAB_TOTAL * 2 * SURF, SURF), 1.0, 6.0, ((1, 64), (2, 16)), jnp.float32)
    less_diag = scatter_about(key_list[2], (2, ENERGIES, SLAB_TOTAL * SLAB_ORBITALS), 1.0, 6.0, ((1, 64), (2, 16)), jnp.float32)
    neighbours = touch_ends(jax.random.randint(key_list[3], (SLAB_TOTAL, 2, NB, SLAB_ORBITALS), 0, SURF), jax.random.fold_in(key_list[3], 1), 0, SURF - 1).astype(jnp.int32)
    hopping = scatter_about(key_list[4], (SLAB_TOTAL, 2, NB, SLAB_ORBITALS), (SLAB_ORBITALS * NB * 4) ** -0.5, 0.046875, ((0, 16),), jnp.float32)
    damp = draw_damp(jax.random.fold_in(key_list[9], 71), 0)
    mode_offset = draw_mode_offset(jax.random.fold_in(key_list[9], 71), 0)
    mode_strength = jnp.clip(jnp.exp(jax.random.uniform(key_list[7], (MODES,), jnp.float32, math.log(0.002), math.log(0.02))), 0.002, 0.02)
    bose = jnp.clip(jnp.exp(jax.random.uniform(key_list[8], (MODES,), jnp.float32, math.log(0.05), math.log(2.0))), 0.05, 2.0)
    return dict(green_rows=green_rows, less_surfaces=less_surfaces, less_diag=less_diag, neighbours=neighbours, hopping=hopping, damp=damp, mode_offset=mode_offset, mode_strength=mode_strength, bose=bose)


PRECISE = lax.Precision.HIGHEST


def coupling_blocks(neighbours, hopping):
    slot_ids = lax.broadcasted_iota(jnp.int32, (1, 1, 1, SURF, 1), 3)
    one_hot = (neighbours[:, :, :, None, :] == slot_ids).astype(jnp.float32)
    return jnp.sum(one_hot * hopping[:, :, :, None, :], axis=2)


def phonon_kernel(mode_offset, mode_strength, bose, energy_count):
    row_ids = lax.broadcasted_iota(jnp.int32, (1, energy_count, energy_count), 1)
    column_ids = lax.broadcasted_iota(jnp.int32, (1, energy_count, energy_count), 2)
    shifts = mode_offset[:, None, None]
    emitted = (column_ids == row_ids + shifts).astype(jnp.float32)
    absorbed = (column_ids == row_ids - shifts).astype(jnp.float32)
    occupied = bose[:, None, None]
    return jnp.sum(mode_strength[:, None, None] * ((occupied + 1.0) * emitted + occupied * absorbed), axis=0)


def complex_product(left_factor, right_factor, pattern):
    real_part = jnp.einsum(pattern, left_factor[0], right_factor[0], precision=PRECISE) - jnp.einsum(pattern, left_factor[1], right_factor[1], precision=PRECISE)
    imag_part = jnp.einsum(pattern, left_factor[0], right_factor[1], precision=PRECISE) + jnp.einsum(pattern, left_factor[1], right_factor[0], precision=PRECISE)
    return jnp.stack([real_part, imag_part])


def block_outer(left_factor, right_factor, surface):
    shape_in = left_factor.shape
    block_count = shape_in[2] // surface
    left_blocks = left_factor.reshape(shape_in[0], shape_in[1], block_count, surface, shape_in[3])
    right_blocks = right_factor.reshape(shape_in[0], shape_in[1], block_count, surface, shape_in[3])
    pattern = "abik,abjk->abij"
    real_part = jnp.einsum(pattern, left_blocks[0], right_blocks[0], precision=PRECISE) + jnp.einsum(pattern, left_blocks[1], right_blocks[1], precision=PRECISE)
    imag_part = jnp.einsum(pattern, left_blocks[1], right_blocks[0], precision=PRECISE) - jnp.einsum(pattern, left_blocks[0], right_blocks[1], precision=PRECISE)
    return jnp.stack([real_part, imag_part]).reshape(shape_in[0], shape_in[1], shape_in[2], surface)


def reference(green_rows, less_surfaces, less_diag, neighbours, hopping, damp, mode_offset, mode_strength, bose):
    couple = coupling_blocks(neighbours, hopping)
    diagonals = less_diag.reshape(2, ENERGIES, SLAB_TOTAL, SLAB_ORBITALS)

    def advance(carried_state, operands):
        rate_row, local_terms = operands
        return rate_row * carried_state + local_terms, carried_state

    final_state, carried = lax.scan(advance, jnp.zeros((2, ENERGIES, SLAB_ORBITALS), jnp.float32), (damp, jnp.moveaxis(diagonals, 2, 0)))
    occupation = diagonals + jnp.moveaxis(carried, 0, 2)
    kernel = phonon_kernel(mode_offset, mode_strength, bose, ENERGIES)
    phonon_sigma = jnp.einsum("ef,cfso->ceso", kernel, occupation, precision=PRECISE)
    surfaces = less_surfaces.reshape(2, ENERGIES, SLAB_TOTAL, 2, SURF, SURF)
    zero_block = jnp.zeros((2, ENERGIES, 1, SURF, SURF), jnp.float32)
    from_lower = jnp.concatenate([zero_block, surfaces[:, :, :-1, 1]], axis=2)
    from_upper = jnp.concatenate([surfaces[:, :, 1:, 0], zero_block], axis=2)
    greens = green_rows.reshape(2, ENERGIES, SLAB_TOTAL, 2 * SURF, SLAB_ORBITALS)

    def one_energy(operands):
        green_now, lower_now, upper_now, sigma_now = operands
        coupled_lower = jnp.einsum("csrj,sqj->csrq", green_now, couple[:, 0], precision=PRECISE)
        coupled_upper = jnp.einsum("csrj,sqj->csrq", green_now, couple[:, 1], precision=PRECISE)
        weighted_lower = complex_product(coupled_lower, lower_now, "srq,sqt->srt")
        weighted_upper = complex_product(coupled_upper, upper_now, "srq,sqt->srt")
        scaled = jnp.stack([
            green_now[0] * sigma_now[0][:, None, :] - green_now[1] * sigma_now[1][:, None, :],
            green_now[0] * sigma_now[1][:, None, :] + green_now[1] * sigma_now[0][:, None, :]])
        left_side = jnp.concatenate([scaled, weighted_lower, weighted_upper], axis=3)
        right_side = jnp.concatenate([green_now, coupled_lower, coupled_upper], axis=3)
        return block_outer(left_side, right_side, SURF)

    per_energy = (jnp.moveaxis(greens, 1, 0), jnp.moveaxis(from_lower, 1, 0), jnp.moveaxis(from_upper, 1, 0), jnp.moveaxis(phonon_sigma, 1, 0))
    blocks = lax.map(one_energy, per_energy)
    correction = jnp.moveaxis(blocks, 0, 1).reshape(2, ENERGIES, SLAB_TOTAL * 2 * SURF, SURF)
    return correction, phonon_sigma.reshape(2, ENERGIES, SLAB_TOTAL * SLAB_ORBITALS)
```

```python
import jax
import jax.numpy as jnp
from jax import lax
from jax.experimental import pallas as pl
from jax.experimental.pallas import tpu as pltpu
from jax.sharding import PartitionSpec as P

MESH = pl.DeviceIdType.MESH
F32 = jnp.float32
BF16 = jnp.bfloat16
NX, NY, NC, NZ = 4, 8, 2, 16
GROUP = 4
ORB = 512
SURF = 128
NB = 8
MODES = 8


def split(value):
    high = value.astype(BF16)
    return high, (value - high.astype(F32)).astype(BF16)


def dot3(left_high, left_low, right_high, right_low, transposed):
    dims = (((1,), (1 if transposed else 0,)), ((), ()))

    def one(left, right):
        return lax.dot_general(left, right, dims, preferred_element_type=F32)

    return one(left_high, right_low) + one(left_low, right_high) + one(left_high, right_high)


def kernel(
    green_hbm, less_hbm, diag_hbm, near_hbm, hop_hbm, damp_hbm, offset_hbm, strength_hbm, bose_hbm,
    out_ref, sigma_ref,
    green, gh, gl, ch, cl, cph, cpl, wh, wl,
    near, hop, damp, diag, offset, strength, bose,
    gathered, stacked, partial, reduced, zout, zgroup, ztotal, low_block, up_block,
    local_sem, xc_sem, y_sem, zs_sem, zr_sem, lead_sem, total_sem, halo_send, halo_recv,
):
    e, s = lax.axis_index("energy"), lax.axis_index("slab")
    x, y, c = e // (NY * NC), lax.rem(e // NC, NY), lax.rem(e, NC)
    lane, group = lax.rem(s, GROUP), s // GROUP

    def at(px, py, pc):
        return (px * NY + py) * NC + pc

    xc_peers = []
    for d in range(1, NX * NC):
        px, pc = lax.rem(x + d // NC, NX), lax.rem(c + d % NC, NC)
        xc_peers.append((at(px, y, pc), s))
    y_peers = [(lax.rem(y + d, NY), (at(x, lax.rem(y + d, NY), c), s)) for d in range(1, NY)]

    barrier = pltpu.get_barrier_semaphore()

    def tell(device):
        pl.semaphore_signal(barrier, inc=1, device_id=device, device_id_type=MESH)

    for _, device in y_peers:
        tell(device)
    for device in xc_peers:
        tell(device)

    @pl.when(s < NZ - 1)
    def _():
        tell((e, s + 1))

    for k in range(GROUP - 1):

        @pl.when(k < lane)
        def _(k=k):
            tell((e, group * GROUP + k))

    for k in range(NZ // GROUP - 1):

        @pl.when(k < group)
        def _(k=k):
            tell((e, jnp.int32(k * GROUP + GROUP - 1)))

    pairs = [
        (diag_hbm, diag), (damp_hbm, damp), (offset_hbm, offset), (strength_hbm, strength), (bose_hbm, bose),
        (near_hbm, near), (hop_hbm, hop), (green_hbm, green),
    ]
    loads = [pltpu.make_async_copy(a, b, local_sem.at[k]) for k, (a, b) in enumerate(pairs)]
    for load in loads:
        load.start()

    leads = jnp.where(lane == GROUP - 1, NZ - GROUP * (group + 1), 0)
    loads[0].wait()
    mine = x * NC + c
    gathered[mine] = diag[...]
    pl.semaphore_wait(barrier, 14 + jnp.where(s > 0, 1, 0) + (GROUP - 1 - lane) + leads)

    for device in xc_peers:
        pltpu.make_async_remote_copy(
            src_ref=diag, dst_ref=gathered.at[mine], send_sem=xc_sem.at[0], recv_sem=xc_sem.at[1],
            device_id=device, device_id_type=MESH,
        ).start()

    to_upper = [
        pltpu.make_async_remote_copy(
            src_ref=less_hbm.at[:, k, pl.ds(SURF, SURF), :], dst_ref=low_block.at[:, k],
            send_sem=halo_send.at[0, k], recv_sem=halo_recv.at[0, k], device_id=(e, s + 1), device_id_type=MESH,
        )
        for k in range(2)
    ]
    to_lower = [
        pltpu.make_async_remote_copy(
            src_ref=less_hbm.at[:, k, pl.ds(0, SURF), :], dst_ref=up_block.at[:, k],
            send_sem=halo_send.at[1, k], recv_sem=halo_recv.at[1, k], device_id=(e, s - 1), device_id_type=MESH,
        )
        for k in range(2)
    ]
    for k in range(2):

        @pl.when(s < NZ - 1)
        def _(k=k):
            to_upper[k].start()

        @pl.when(s > 0)
        def _(k=k):
            to_lower[k].start()

    @pl.when(s == 0)
    def _():
        low_block[...] = jnp.zeros_like(low_block)

    @pl.when(s == NZ - 1)
    def _():
        up_block[...] = jnp.zeros_like(up_block)

    for load in loads[1:5]:
        load.wait()
    rows = lax.broadcasted_iota(jnp.int32, (16, 16), 0)
    cols = lax.broadcasted_iota(jnp.int32, (16, 16), 1)
    energy_to = x * 32 + (rows // 2) * 4 + c * 2 + lax.rem(rows, 2)
    energy_from = (cols // 4) * 32 + y * 4 + lax.rem(cols, 4)
    gap = energy_from - energy_to
    coupling = jnp.zeros((16, 16), F32)
    for q in range(MODES):
        emitted = (gap == offset[q]).astype(F32)
        absorbed = (gap == -offset[q]).astype(F32)
        coupling = coupling + strength[q] * ((bose[q] + 1.0) * emitted + bose[q] * absorbed)

    loads[5].wait()
    loads[6].wait()
    slots = lax.broadcasted_iota(jnp.int32, (SURF, ORB), 0)
    for t in range(2):
        couple = jnp.zeros((SURF, ORB), F32)
        for k in range(NB):
            couple = couple + jnp.where(near[0, t, k : k + 1, :] == slots, hop[0, t, k : k + 1, :], 0.0)
        cph[pl.ds(t * SURF, SURF)], cpl[pl.ds(t * SURF, SURF)] = split(couple)
    loads[7].wait()
    for k in range(2):
        for b in range(2):
            for part in range(2):
                high, low = split(green[part, k, pl.ds(b * SURF, SURF), :])
                gh[k, b, pl.ds(part * SURF, SURF), :] = high
                gl[k, b, pl.ds(part * SURF, SURF), :] = low

    def arrived(buffer, count, sem):
        pltpu.make_async_copy(buffer.at[pl.ds(0, count)], buffer.at[pl.ds(0, count)], sem).wait()

    arrived(gathered, 7, xc_sem.at[0])
    arrived(gathered, 7, xc_sem.at[1])
    for j in range(8):
        for part in range(2):
            stacked[pl.ds(2 * j, 2), pl.ds(part * ORB, ORB)] = gathered[j, part]
    product = jnp.dot(coupling, stacked[...], precision=lax.Precision.HIGHEST, preferred_element_type=F32)
    for j in range(NY):
        partial[j] = product[2 * j : 2 * j + 2, :]
    for there, device in y_peers:
        pltpu.make_async_remote_copy(
            src_ref=partial.at[there], dst_ref=reduced.at[y], send_sem=y_sem.at[0], recv_sem=y_sem.at[1],
            device_id=device, device_id_type=MESH,
        ).start()
    reduced[y] = partial[y]

    for k in range(2):
        for b in range(2):
            high, low = split(dot3(gh[k, b], gl[k, b], cph[...], cpl[...], True))
            ch[k, b], cl[k, b] = high, low

    def surfaces(k):
        @pl.when(s > 0)
        def _():
            to_upper[k].wait_recv()

        @pl.when(s < NZ - 1)
        def _():
            to_lower[k].wait_recv()

        for t, block in ((0, low_block), (1, up_block)):
            real_high, real_low = split(block[0, k])
            imag_high, imag_low = split(block[1, k])

            def matrix(real, imag):
                return jnp.concatenate(
                    [jnp.concatenate([real, imag], axis=1), jnp.concatenate([-imag, real], axis=1)], axis=0
                )

            right_high, right_low = matrix(real_high, imag_high), matrix(real_low, imag_low)
            for b in range(2):

                def side(ref):
                    lanes = pl.ds(t * SURF, SURF)
                    return jnp.concatenate([ref[k, b, pl.ds(0, SURF), lanes], ref[k, b, pl.ds(SURF, SURF), lanes]], axis=1)

                high, low = split(dot3(side(ch), side(cl), right_high, right_low, False))
                for part in range(2):
                    there = (b, pl.ds(part * SURF, SURF), pl.ds(t * SURF, SURF))
                    wh[there] = high[:, part * SURF : (part + 1) * SURF]
                    wl[there] = low[:, part * SURF : (part + 1) * SURF]
        for b in range(2):
            quad = dot3(wh[b], wl[b], ch[k, b], cl[k, b], True)
            here = pl.ds(b * SURF, SURF)
            out_ref[0, k, here, :] = quad[:SURF, :SURF] + quad[SURF:, SURF:]
            out_ref[1, k, here, :] = quad[SURF:, :SURF] - quad[:SURF, SURF:]

    surfaces(0)

    arrived(partial, 7, y_sem.at[0])
    arrived(reduced, 7, y_sem.at[1])
    own = reduced[0]
    for j in range(1, NY):
        own = own + reduced[j]
    wide = 2 * ORB
    rate = jnp.broadcast_to(damp[...], (2, ORB))
    zout[0, :, pl.ds(0, wide)] = own
    zout[0, :, pl.ds(wide, ORB)] = rate
    in_group = [
        pltpu.make_async_remote_copy(
            src_ref=zout.at[0], dst_ref=zgroup.at[lane], send_sem=zs_sem.at[k], recv_sem=zr_sem.at[lane],
            device_id=(e, group * GROUP + k), device_id_type=MESH,
        )
        for k in range(1, GROUP)
    ]
    for k in range(1, GROUP):

        @pl.when(k > lane)
        def _(k=k):
            in_group[k - 1].start()

    surfaces(1)

    def from_slot(buffer, sems, k):
        return pltpu.make_async_copy(buffer.at[k], buffer.at[k], sems.at[k])

    def twice(value):
        return jnp.concatenate([value, value], axis=1)

    def gather_step(k, state):
        carried, decay = state
        from_slot(zgroup, zr_sem, k).wait()
        row = zgroup[k]
        step = row[:, wide:]
        return carried * twice(step) + row[:, :wide], decay * step

    carried, decay = lax.fori_loop(0, lane, gather_step, (jnp.zeros((2, wide), F32), jnp.ones((2, ORB), F32)))
    totals = [
        pltpu.make_async_remote_copy(
            src_ref=zout.at[1], dst_ref=ztotal.at[group], send_sem=lead_sem.at[k], recv_sem=total_sem.at[group],
            device_id=(e, jnp.int32(k)), device_id_type=MESH,
        )
        for k in range(GROUP, NZ)
    ]

    @pl.when(lane == GROUP - 1)
    def _():
        zout[1, :, pl.ds(0, wide)] = carried * twice(rate) + own
        zout[1, :, pl.ds(wide, ORB)] = decay * rate

    for k in range(NZ - 1, GROUP - 1, -1):

        @pl.when((lane == GROUP - 1) & (k // GROUP > group))
        def _(k=k):
            totals[k - GROUP].start()

    def total_step(k, total):
        from_slot(ztotal, total_sem, k).wait()
        row = ztotal[k]
        return total * twice(row[:, wide:]) + row[:, :wide]

    below = lax.fori_loop(0, group, total_step, jnp.zeros((2, wide), F32))
    sigma = own + carried + twice(decay) * below
    for part in range(2):
        sigma_ref[part] = sigma[:, part * ORB : (part + 1) * ORB]

    for k in range(2):
        sigma_real, sigma_imag = sigma[k : k + 1, :ORB], sigma[k : k + 1, ORB:]
        for b in range(2):
            here = pl.ds(b * SURF, SURF)
            green_real, green_imag = green[0, k, here, :], green[1, k, here, :]
            real_high, real_low = split(green_real * sigma_real - green_imag * sigma_imag)
            imag_high, imag_low = split(green_real * sigma_imag + green_imag * sigma_real)
            quad = dot3(
                jnp.concatenate([real_high, imag_high], axis=0), jnp.concatenate([real_low, imag_low], axis=0),
                gh[k, b], gl[k, b], True,
            )
            out_ref[0, k, here, :] += quad[:SURF, :SURF] + quad[SURF:, SURF:]
            out_ref[1, k, here, :] += quad[SURF:, :SURF] - quad[:SURF, SURF:]

    for k in range(1, GROUP):

        @pl.when(k > lane)
        def _(k=k):
            in_group[k - 1].wait_send()

    for k in range(GROUP, NZ):

        @pl.when((lane == GROUP - 1) & (k // GROUP > group))
        def _(k=k):
            totals[k - GROUP].wait_send()

    for k in range(2):

        @pl.when(s < NZ - 1)
        def _(k=k):
            to_upper[k].wait_send()

        @pl.when(s > 0)
        def _(k=k):
            to_lower[k].wait_send()


def local(*args):
    vmem, smem, dma = pltpu.VMEM, pltpu.SMEM, pltpu.SemaphoreType.DMA
    return pl.pallas_call(
        kernel,
        out_shape=(
            jax.ShapeDtypeStruct((2, 2, 2 * SURF, SURF), F32),
            jax.ShapeDtypeStruct((2, 2, ORB), F32),
        ),
        in_specs=[pl.BlockSpec(memory_space=pltpu.HBM)] * 9,
        out_specs=(pl.BlockSpec(memory_space=vmem), pl.BlockSpec(memory_space=vmem)),
        scratch_shapes=[
            vmem((2, 2, 2 * SURF, ORB), F32),
            vmem((2, 2, 2 * SURF, ORB), BF16),
            vmem((2, 2, 2 * SURF, ORB), BF16),
            vmem((2, 2, 2 * SURF, 2 * SURF), BF16),
            vmem((2, 2, 2 * SURF, 2 * SURF), BF16),
            vmem((2 * SURF, ORB), BF16),
            vmem((2 * SURF, ORB), BF16),
            vmem((2, 2 * SURF, 2 * SURF), BF16),
            vmem((2, 2 * SURF, 2 * SURF), BF16),
            vmem((1, 2, NB, ORB), jnp.int32),
            vmem((1, 2, NB, ORB), F32),
            vmem((1, ORB), F32),
            vmem((2, 2, ORB), F32),
            smem((MODES,), jnp.int32),
            smem((MODES,), F32),
            smem((MODES,), F32),
            vmem((8, 2, 2, ORB), F32),
            vmem((16, 2 * ORB), F32),
            vmem((NY, 2, 2 * ORB), F32),
            vmem((NY, 2, 2 * ORB), F32),
            vmem((2, 2, 3 * ORB), F32),
            vmem((GROUP, 2, 3 * ORB), F32),
            vmem((NZ // GROUP, 2, 3 * ORB), F32),
            vmem((2, 2, SURF, SURF), F32),
            vmem((2, 2, SURF, SURF), F32),
            dma((8,)),
            dma((2,)),
            dma((2,)),
            dma((GROUP,)),
            dma((GROUP,)),
            dma((NZ,)),
            dma((NZ // GROUP,)),
            dma((2, 2)),
            dma((2, 2)),
        ],
        compiler_params=pltpu.CompilerParams(
            collective_id=0, has_side_effects=True, vmem_limit_bytes=48 * 1024 * 1024
        ),
        cost_estimate=pl.CostEstimate(flops=5_000_000_000, bytes_accessed=4_000_000, transcendentals=0),
    )(*(pltpu.with_memory_space_constraint(arg, pltpu.HBM) for arg in args))


def solution(mesh):
    placed = (
        P(None, "energy", "slab", None),
        P(None, "energy", "slab", None),
        P(None, "energy", "slab"),
        P("slab", None, None, None),
        P("slab", None, None, None),
        P("slab", None),
        P(),
        P(),
        P(),
    )
    return jax.shard_map(
        local,
        mesh=mesh,
        in_specs=placed,
        out_specs=(P(None, "energy", "slab", None), P(None, "energy", "slab")),
        check_vma=False,
    )
```

```python
import jax
import jax.numpy as jnp
from jax import lax
from jax.experimental import pallas as pl
from jax.experimental.pallas import tpu as pltpu
from jax.sharding import PartitionSpec as P

MESH = pl.DeviceIdType.MESH
F32 = jnp.float32
BF16 = jnp.bfloat16
NX, NY, NC, NZ = 4, 8, 2, 16
REACH = 8
ORB = 512
SURF = 128
NB = 8
MODES = 8


def split(value):
    high = value.astype(BF16)
    return high, (value - high.astype(F32)).astype(BF16)


def dot3(left_high, left_low, right_high, right_low, transposed):
    dims = (((1,), (1 if transposed else 0,)), ((), ()))

    def one(left, right):
        return lax.dot_general(left, right, dims, preferred_element_type=F32)

    return one(left_high, right_low) + one(left_low, right_high) + one(left_high, right_high)


def kernel(
    green_hbm, less_hbm, diag_hbm, near_hbm, hop_hbm, damp_hbm, offset_hbm, strength_hbm, bose_hbm,
    out_ref, sigma_ref,
    green, gh, gl, ch, cl, cph, cpl, wh, wl,
    near, hop, damp, diag, offset, strength, bose,
    gathered, stacked, partial, reduced, zout, zin, before, low_block, up_block,
    local_sem, xc_sem, y_sem, zs_sem, zr_sem, halo_send, halo_recv, down_sem, up_sem,
):
    e, s = lax.axis_index("energy"), lax.axis_index("slab")
    x, y, c = e // (NY * NC), lax.rem(e // NC, NY), lax.rem(e, NC)

    def at(px, py, pc):
        return (px * NY + py) * NC + pc

    xc_peers = []
    for d in range(1, NX * NC):
        px, pc = lax.rem(x + d // NC, NX), lax.rem(c + d % NC, NC)
        xc_peers.append((at(px, y, pc), s))
    y_peers = [(lax.rem(y + d, NY), (at(x, lax.rem(y + d, NY), c), s)) for d in range(1, NY)]

    barrier = pltpu.get_barrier_semaphore()

    def tell(device):
        pl.semaphore_signal(barrier, inc=1, device_id=device, device_id_type=MESH)

    for _, device in y_peers:
        tell(device)
    for device in xc_peers:
        tell(device)

    @pl.when(s < NZ - 1)
    def _():
        tell((e, s + 1))

    @pl.when(s > 0)
    def _():
        tell((e, s - 1))

    pairs = [
        (diag_hbm, diag), (damp_hbm, damp), (offset_hbm, offset), (strength_hbm, strength), (bose_hbm, bose),
        (near_hbm, near), (hop_hbm, hop), (green_hbm, green),
    ]
    loads = [pltpu.make_async_copy(a, b, local_sem.at[k]) for k, (a, b) in enumerate(pairs)]
    for load in loads:
        load.start()

    loads[0].wait()
    mine = x * NC + c
    gathered[mine] = diag[...]
    pl.semaphore_wait(barrier, 14 + jnp.where(s > 0, 1, 0) + jnp.where(s < NZ - 1, 1, 0))

    for device in xc_peers:
        pltpu.make_async_remote_copy(
            src_ref=diag, dst_ref=gathered.at[mine], send_sem=xc_sem.at[0], recv_sem=xc_sem.at[1],
            device_id=device, device_id_type=MESH,
        ).start()

    to_upper = [
        pltpu.make_async_remote_copy(
            src_ref=less_hbm.at[:, k, pl.ds(SURF, SURF), :], dst_ref=low_block.at[:, k],
            send_sem=halo_send.at[0, k], recv_sem=halo_recv.at[0, k], device_id=(e, s + 1), device_id_type=MESH,
        )
        for k in range(2)
    ]
    to_lower = [
        pltpu.make_async_remote_copy(
            src_ref=less_hbm.at[:, k, pl.ds(0, SURF), :], dst_ref=up_block.at[:, k],
            send_sem=halo_send.at[1, k], recv_sem=halo_recv.at[1, k], device_id=(e, s - 1), device_id_type=MESH,
        )
        for k in range(2)
    ]
    for k in range(2):

        @pl.when(s < NZ - 1)
        def _(k=k):
            to_upper[k].start()

        @pl.when(s > 0)
        def _(k=k):
            to_lower[k].start()

    def pass_on(sem, step, when, there):
        @pl.when(when)
        def _():
            pl.semaphore_signal(sem.at[step], inc=1, device_id=(e, there), device_id_type=MESH)

    def hear(sem, step, when):
        @pl.when(when)
        def _():
            pl.semaphore_wait(sem.at[step], 1)

    pass_on(down_sem, 0, (s >= 1) & (s <= NZ - 2), s - 1)
    pass_on(up_sem, 0, (s >= 1) & (s <= NZ - 2), s + 1)

    @pl.when(s == 0)
    def _():
        low_block[...] = jnp.zeros_like(low_block)

    @pl.when(s == NZ - 1)
    def _():
        up_block[...] = jnp.zeros_like(up_block)

    for load in loads[1:5]:
        load.wait()
    rows = lax.broadcasted_iota(jnp.int32, (16, 16), 0)
    cols = lax.broadcasted_iota(jnp.int32, (16, 16), 1)
    energy_to = x * 32 + (rows // 2) * 4 + c * 2 + lax.rem(rows, 2)
    energy_from = (cols // 4) * 32 + y * 4 + lax.rem(cols, 4)
    gap = energy_from - energy_to
    coupling = jnp.zeros((16, 16), F32)
    for q in range(MODES):
        emitted = (gap == offset[q]).astype(F32)
        absorbed = (gap == -offset[q]).astype(F32)
        coupling = coupling + strength[q] * ((bose[q] + 1.0) * emitted + bose[q] * absorbed)

    loads[5].wait()
    loads[6].wait()
    slots = lax.broadcasted_iota(jnp.int32, (SURF, ORB), 0)
    for t in range(2):
        couple = jnp.zeros((SURF, ORB), F32)
        for k in range(NB):
            couple = couple + jnp.where(near[0, t, k : k + 1, :] == slots, hop[0, t, k : k + 1, :], 0.0)
        cph[pl.ds(t * SURF, SURF)], cpl[pl.ds(t * SURF, SURF)] = split(couple)
    loads[7].wait()
    for k in range(2):
        for b in range(2):
            for part in range(2):
                high, low = split(green[part, k, pl.ds(b * SURF, SURF), :])
                gh[k, b, pl.ds(part * SURF, SURF), :] = high
                gl[k, b, pl.ds(part * SURF, SURF), :] = low

    hear(down_sem, 0, s <= NZ - 3)
    hear(up_sem, 0, s >= 2)
    pass_on(down_sem, 1, (s >= 2) & (s <= NZ - 2), s - 2)
    pass_on(up_sem, 1, (s >= 2) & (s <= NZ - 3), s + 2)

    def arrived(buffer, count, sem):
        pltpu.make_async_copy(buffer.at[pl.ds(0, count)], buffer.at[pl.ds(0, count)], sem).wait()

    arrived(gathered, 7, xc_sem.at[0])
    arrived(gathered, 7, xc_sem.at[1])
    for j in range(8):
        for part in range(2):
            stacked[pl.ds(2 * j, 2), pl.ds(part * ORB, ORB)] = gathered[j, part]
    product = jnp.dot(coupling, stacked[...], precision=lax.Precision.HIGHEST, preferred_element_type=F32)
    for j in range(NY):
        partial[j] = product[2 * j : 2 * j + 2, :]
    for there, device in y_peers:
        pltpu.make_async_remote_copy(
            src_ref=partial.at[there], dst_ref=reduced.at[y], send_sem=y_sem.at[0], recv_sem=y_sem.at[1],
            device_id=device, device_id_type=MESH,
        ).start()
    reduced[y] = partial[y]

    for k in range(2):
        for b in range(2):
            high, low = split(dot3(gh[k, b], gl[k, b], cph[...], cpl[...], True))
            ch[k, b], cl[k, b] = high, low

    def surfaces(k):
        @pl.when(s > 0)
        def _():
            to_upper[k].wait_recv()

        @pl.when(s < NZ - 1)
        def _():
            to_lower[k].wait_recv()

        for t, block in ((0, low_block), (1, up_block)):
            real_high, real_low = split(block[0, k])
            imag_high, imag_low = split(block[1, k])

            def matrix(real, imag):
                return jnp.concatenate(
                    [jnp.concatenate([real, imag], axis=1), jnp.concatenate([-imag, real], axis=1)], axis=0
                )

            right_high, right_low = matrix(real_high, imag_high), matrix(real_low, imag_low)
            for b in range(2):

                def side(ref):
                    lanes = pl.ds(t * SURF, SURF)
                    return jnp.concatenate([ref[k, b, pl.ds(0, SURF), lanes], ref[k, b, pl.ds(SURF, SURF), lanes]], axis=1)

                high, low = split(dot3(side(ch), side(cl), right_high, right_low, False))
                for part in range(2):
                    there = (b, pl.ds(part * SURF, SURF), pl.ds(t * SURF, SURF))
                    wh[there] = high[:, part * SURF : (part + 1) * SURF]
                    wl[there] = low[:, part * SURF : (part + 1) * SURF]
        for b in range(2):
            quad = dot3(wh[b], wl[b], ch[k, b], cl[k, b], True)
            here = pl.ds(b * SURF, SURF)
            out_ref[0, k, here, :] = quad[:SURF, :SURF] + quad[SURF:, SURF:]
            out_ref[1, k, here, :] = quad[SURF:, :SURF] - quad[:SURF, SURF:]

    hear(down_sem, 1, s <= NZ - 4)
    hear(up_sem, 1, s >= 4)
    pass_on(down_sem, 2, (s >= 4) & (s <= NZ - 2), s - 4)

    surfaces(0)
    surfaces(1)

    arrived(partial, 7, y_sem.at[0])
    arrived(reduced, 7, y_sem.at[1])
    own = reduced[0]
    for j in range(1, NY):
        own = own + reduced[j]
    wide = 2 * ORB
    rate = jnp.broadcast_to(damp[...], (2, ORB))
    zout[0, :, pl.ds(0, wide)] = own
    zout[0, :, pl.ds(wide, ORB)] = rate
    ahead = [
        pltpu.make_async_remote_copy(
            src_ref=zout.at[0 if d < REACH else 1], dst_ref=zin.at[d - 1], send_sem=zs_sem.at[d - 1],
            recv_sem=zr_sem.at[d - 1], device_id=(e, s + d), device_id_type=MESH,
        )
        for d in range(1, REACH + 1)
    ]

    def each_ahead(distances, act):
        for d in distances:

            @pl.when(s + d < NZ)
            def _(d=d):
                act(ahead[d - 1])

    each_ahead(range(1, 5), lambda copy: copy.start())
    hear(down_sem, 2, s <= NZ - 6)
    each_ahead(range(5, REACH), lambda copy: copy.start())

    def from_slot(k):
        return pltpu.make_async_copy(zin.at[k], zin.at[k], zr_sem.at[k])

    def twice(value):
        return jnp.concatenate([value, value], axis=1)

    before[...] = jnp.zeros_like(before)

    @pl.when(s >= REACH)
    def _():
        from_slot(REACH - 1).wait()
        before[...] = zin[REACH - 1, :, pl.ds(0, wide)]

    near_count = jnp.minimum(s, REACH - 1)

    def scan_step(k, carried):
        slot = near_count - 1 - k
        from_slot(slot).wait()
        row = zin[slot]
        return carried * twice(row[:, wide:]) + row[:, :wide]

    carried = lax.fori_loop(0, near_count, scan_step, before[...])
    zout[1, :, pl.ds(0, wide)] = carried * twice(rate) + own
    zout[1, :, pl.ds(wide, ORB)] = rate
    each_ahead((REACH,), lambda copy: copy.start())
    sigma = own + carried
    for part in range(2):
        sigma_ref[part] = sigma[:, part * ORB : (part + 1) * ORB]

    for k in range(2):
        sigma_real, sigma_imag = sigma[k : k + 1, :ORB], sigma[k : k + 1, ORB:]
        for b in range(2):
            here = pl.ds(b * SURF, SURF)
            green_real, green_imag = green[0, k, here, :], green[1, k, here, :]
            real_high, real_low = split(green_real * sigma_real - green_imag * sigma_imag)
            imag_high, imag_low = split(green_real * sigma_imag + green_imag * sigma_real)
            quad = dot3(
                jnp.concatenate([real_high, imag_high], axis=0), jnp.concatenate([real_low, imag_low], axis=0),
                gh[k, b], gl[k, b], True,
            )
            out_ref[0, k, here, :] += quad[:SURF, :SURF] + quad[SURF:, SURF:]
            out_ref[1, k, here, :] += quad[SURF:, :SURF] - quad[:SURF, SURF:]

    each_ahead(range(1, REACH + 1), lambda copy: copy.wait_send())

    for k in range(2):

        @pl.when(s < NZ - 1)
        def _(k=k):
            to_upper[k].wait_send()

        @pl.when(s > 0)
        def _(k=k):
            to_lower[k].wait_send()


def store(out_ref, sigma_ref, out_hbm, sigma_hbm, sem):
    copies = [
        pltpu.make_async_copy(out_ref, out_hbm, sem.at[0]),
        pltpu.make_async_copy(sigma_ref, sigma_hbm, sem.at[1]),
    ]
    for copy in copies:
        copy.start()
    for copy in copies:
        copy.wait()


def local(*args):
    vmem, smem, dma = pltpu.VMEM, pltpu.SMEM, pltpu.SemaphoreType.DMA
    shapes = (jax.ShapeDtypeStruct((2, 2, 2 * SURF, SURF), F32), jax.ShapeDtypeStruct((2, 2, ORB), F32))
    results = pl.pallas_call(
        kernel,
        out_shape=shapes,
        in_specs=[pl.BlockSpec(memory_space=pltpu.HBM)] * 9,
        out_specs=(pl.BlockSpec(memory_space=vmem), pl.BlockSpec(memory_space=vmem)),
        scratch_shapes=[
            vmem((2, 2, 2 * SURF, ORB), F32),
            vmem((2, 2, 2 * SURF, ORB), BF16),
            vmem((2, 2, 2 * SURF, ORB), BF16),
            vmem((2, 2, 2 * SURF, 2 * SURF), BF16),
            vmem((2, 2, 2 * SURF, 2 * SURF), BF16),
            vmem((2 * SURF, ORB), BF16),
            vmem((2 * SURF, ORB), BF16),
            vmem((2, 2 * SURF, 2 * SURF), BF16),
            vmem((2, 2 * SURF, 2 * SURF), BF16),
            vmem((1, 2, NB, ORB), jnp.int32),
            vmem((1, 2, NB, ORB), F32),
            vmem((1, ORB), F32),
            vmem((2, 2, ORB), F32),
            smem((MODES,), jnp.int32),
            smem((MODES,), F32),
            smem((MODES,), F32),
            vmem((8, 2, 2, ORB), F32),
            vmem((16, 2 * ORB), F32),
            vmem((NY, 2, 2 * ORB), F32),
            vmem((NY, 2, 2 * ORB), F32),
            vmem((2, 2, 3 * ORB), F32),
            vmem((REACH, 2, 3 * ORB), F32),
            vmem((2, 2 * ORB), F32),
            vmem((2, 2, SURF, SURF), F32),
            vmem((2, 2, SURF, SURF), F32),
            dma((8,)),
            dma((2,)),
            dma((2,)),
            dma((REACH,)),
            dma((REACH,)),
            dma((2, 2)),
            dma((2, 2)),
            pltpu.SemaphoreType.REGULAR((3,)),
            pltpu.SemaphoreType.REGULAR((2,)),
        ],
        compiler_params=pltpu.CompilerParams(
            collective_id=0, has_side_effects=True, vmem_limit_bytes=48 * 1024 * 1024
        ),
        cost_estimate=pl.CostEstimate(flops=5_000_000_000, bytes_accessed=4_000_000, transcendentals=0),
    )(*(pltpu.with_memory_space_constraint(arg, pltpu.HBM) for arg in args))
    return pl.pallas_call(
        store,
        out_shape=shapes,
        in_specs=[pl.BlockSpec(memory_space=vmem)] * 2,
        out_specs=[pl.BlockSpec(memory_space=pl.ANY)] * 2,
        scratch_shapes=[dma((2,))],
    )(*(pltpu.with_memory_space_constraint(result, vmem) for result in results))


def solution(mesh):
    placed = (
        P(None, "energy", "slab", None),
        P(None, "energy", "slab", None),
        P(None, "energy", "slab"),
        P("slab", None, None, None),
        P("slab", None, None, None),
        P("slab", None),
        P(),
        P(),
        P(),
    )
    return jax.shard_map(
        local,
        mesh=mesh,
        in_specs=placed,
        out_specs=(P(None, "energy", "slab", None), P(None, "energy", "slab")),
        check_vma=False,
    )
```

```python
import jax
import jax.numpy as jnp
from jax import lax
from jax.experimental import pallas as pl
from jax.experimental.pallas import tpu as pltpu
from jax.sharding import PartitionSpec as P

MESH = pl.DeviceIdType.MESH
F32 = jnp.float32
BF16 = jnp.bfloat16
NX, NY, NC, NZ = 4, 8, 2, 16
REACH = 8
NEAR = 3
LATE = NZ - 4
HALF = 8
ORB = 512
SURF = 128
NB = 8
MODES = 8


def split(value):
    high = value.astype(BF16)
    return high, (value - high.astype(F32)).astype(BF16)


def dot3(left_high, left_low, right_high, right_low, transposed):
    dims = (((1,), (1 if transposed else 0,)), ((), ()))

    def one(left, right):
        return lax.dot_general(left, right, dims, preferred_element_type=F32)

    return one(left_high, right_low) + one(left_low, right_high) + one(left_high, right_high)


def kernel(
    green_hbm, less_hbm, diag_hbm, near_hbm, hop_hbm, damp_hbm, offset_hbm, strength_hbm, bose_hbm,
    out_ref, sigma_ref,
    green, gh, gl, ch, cl, cph, cpl, wh, wl,
    near, hop, damp, diag, offset, strength, bose,
    gathered, stacked, partial, reduced, zout, zin, damp_in, before, low_block, up_block,
    local_sem, xc_sem, y_sem, zs_sem, zr_sem, ds_sem, dr_sem, halo_send, halo_recv, down_sem, up_sem, ring_sem,
):
    e, s = lax.axis_index("energy"), lax.axis_index("slab")
    x, y, c = e // (NY * NC), lax.rem(e // NC, NY), lax.rem(e, NC)

    def at(px, py, pc):
        return (px * NY + py) * NC + pc

    xc_peers = []
    for d in (4, 5, 2, 3, 6, 7, 1):
        px, pc = lax.rem(x + d // NC, NX), lax.rem(c + d % NC, NC)
        xc_peers.append((at(px, y, pc), s))
    y_peers = [(lax.rem(y + d, NY), (at(x, lax.rem(y + d, NY), c), s)) for d in range(1, NY)]

    barrier = pltpu.get_barrier_semaphore()

    def tell(device):
        pl.semaphore_signal(barrier, inc=1, device_id=device, device_id_type=MESH)

    pairs = [
        (diag_hbm, diag), (damp_hbm, damp), (offset_hbm, offset), (strength_hbm, strength), (bose_hbm, bose),
        (near_hbm, near), (hop_hbm, hop), (green_hbm, green),
    ]
    loads = [pltpu.make_async_copy(a, b, local_sem.at[k]) for k, (a, b) in enumerate(pairs)]
    loads[0].start()
    for device in xc_peers:
        tell(device)
    for d in (1, NY - 1):
        tell(y_peers[d - 1][1])

    @pl.when(s < NZ - 1)
    def _():
        tell((e, s + 1))

    @pl.when(s > 0)
    def _():
        tell((e, s - 1))

    loads[0].wait()
    mine = x * NC + c
    gathered[mine] = diag[...]
    pl.semaphore_wait(barrier, 9 + jnp.where(s > 0, 1, 0) + jnp.where(s < NZ - 1, 1, 0))

    for device in xc_peers:
        pltpu.make_async_remote_copy(
            src_ref=diag, dst_ref=gathered.at[mine], send_sem=xc_sem.at[0], recv_sem=xc_sem.at[1],
            device_id=device, device_id_type=MESH,
        ).start()

    to_upper = [
        pltpu.make_async_remote_copy(
            src_ref=less_hbm.at[:, k, pl.ds(SURF, SURF), :], dst_ref=low_block.at[:, k],
            send_sem=halo_send.at[0, k], recv_sem=halo_recv.at[0, k], device_id=(e, s + 1), device_id_type=MESH,
        )
        for k in range(2)
    ]
    to_lower = [
        pltpu.make_async_remote_copy(
            src_ref=less_hbm.at[:, k, pl.ds(0, SURF), :], dst_ref=up_block.at[:, k],
            send_sem=halo_send.at[1, k], recv_sem=halo_recv.at[1, k], device_id=(e, s - 1), device_id_type=MESH,
        )
        for k in range(2)
    ]
    for k in range(2):

        @pl.when(s < NZ - 1)
        def _(k=k):
            to_upper[k].start()

        @pl.when(s > 0)
        def _(k=k):
            to_lower[k].start()

    for load in loads[1:]:
        load.start()

    def pass_on(sem, step, when, there):
        @pl.when(when)
        def _():
            pl.semaphore_signal(sem.at[step], inc=1, device_id=(e, there), device_id_type=MESH)

    def hear(sem, step, when):
        @pl.when(when)
        def _():
            pl.semaphore_wait(sem.at[step], 1)

    def ring_round(step):
        for way, d in ((0, step), (1, NY - step)):
            pl.semaphore_signal(ring_sem.at[step - 1, way], inc=1, device_id=y_peers[d - 1][1], device_id_type=MESH)

    def ring_wait(step):
        for way in range(2):
            pl.semaphore_wait(ring_sem.at[step - 1, way], 1)

    ring_round(1)
    pass_on(down_sem, 0, (s >= 1) & (s <= NZ - 2), s - 1)
    pass_on(up_sem, 0, (s >= 1) & (s <= NZ - 2), s + 1)

    @pl.when(s == 0)
    def _():
        low_block[...] = jnp.zeros_like(low_block)

    @pl.when(s == NZ - 1)
    def _():
        up_block[...] = jnp.zeros_like(up_block)

    for load in loads[1:5]:
        load.wait()
    rows = lax.broadcasted_iota(jnp.int32, (16, 16), 0)
    cols = lax.broadcasted_iota(jnp.int32, (16, 16), 1)
    energy_to = x * 32 + (rows // 2) * 4 + c * 2 + lax.rem(rows, 2)
    energy_from = (cols // 4) * 32 + y * 4 + lax.rem(cols, 4)
    gap = energy_from - energy_to
    coupling = jnp.zeros((16, 16), F32)
    for q in range(MODES):
        emitted = (gap == offset[q]).astype(F32)
        absorbed = (gap == -offset[q]).astype(F32)
        coupling = coupling + strength[q] * ((bose[q] + 1.0) * emitted + bose[q] * absorbed)

    loads[5].wait()
    loads[6].wait()
    slots = lax.broadcasted_iota(jnp.int32, (SURF, ORB), 0)
    for t in range(2):
        couple = jnp.zeros((SURF, ORB), F32)
        for k in range(NB):
            couple = couple + jnp.where(near[0, t, k : k + 1, :] == slots, hop[0, t, k : k + 1, :], 0.0)
        cph[pl.ds(t * SURF, SURF)], cpl[pl.ds(t * SURF, SURF)] = split(couple)
    loads[7].wait()
    for k in range(2):
        for b in range(2):
            for part in range(2):
                high, low = split(green[part, k, pl.ds(b * SURF, SURF), :])
                gh[k, b, pl.ds(part * SURF, SURF), :] = high
                gl[k, b, pl.ds(part * SURF, SURF), :] = low

    ring_wait(1)
    ring_round(2)
    hear(down_sem, 0, s <= NZ - 3)
    hear(up_sem, 0, s >= 2)
    pass_on(down_sem, 1, (s >= 2) & (s <= NZ - 2), s - 2)
    pass_on(up_sem, 1, (s >= LATE - 3) & (s <= NZ - 4), s + 2)

    def arrived(buffer, count, sem):
        pltpu.make_async_copy(buffer.at[pl.ds(0, count)], buffer.at[pl.ds(0, count)], sem).wait()

    arrived(gathered, 7, xc_sem.at[1])
    for j in range(8):
        for part in range(2):
            stacked[pl.ds(2 * j, 2), pl.ds(part * ORB, ORB)] = gathered[j, part]
    product = jnp.dot(coupling, stacked[...], precision=lax.Precision.HIGHEST, preferred_element_type=F32)
    for j in range(NY):
        partial[j] = product[2 * j : 2 * j + 2, :]
    ring_wait(2)
    for d in (4, 3, 5, 2, 6, 1, 7):
        there, device = y_peers[d - 1]
        pltpu.make_async_remote_copy(
            src_ref=partial.at[there], dst_ref=reduced.at[y], send_sem=y_sem.at[0], recv_sem=y_sem.at[1],
            device_id=device, device_id_type=MESH,
        ).start()
    reduced[y] = partial[y]

    hear(down_sem, 1, s <= NZ - 4)
    hear(up_sem, 1, (s >= LATE - 1) & (s <= NZ - 2))
    pass_on(down_sem, 2, (s >= LATE - 1) & (s <= NZ - 2), s - 4)
    damps = [
        pltpu.make_async_remote_copy(
            src_ref=damp, dst_ref=damp_in.at[d - 1], send_sem=ds_sem.at[d - 1], recv_sem=dr_sem.at[d - 1],
            device_id=(e, s + d), device_id_type=MESH,
        )
        for d in range(1, REACH)
    ]

    def each_ahead(copies, distances, act):
        for d in distances:

            @pl.when((s + d < NZ) & ((d <= NEAR) | (s >= HALF)))
            def _(d=d):
                act(copies[d - 1])

    def each_carry(distances, act):
        for d in distances:

            @pl.when((s == HALF - 1) | ((d == 4) & (s < HALF)))
            def _(d=d):
                act(carries[d - 4])

    each_ahead(damps, range(1, 5), lambda copy: copy.start())

    for k in range(2):
        for b in range(2):
            high, low = split(dot3(gh[k, b], gl[k, b], cph[...], cpl[...], True))
            ch[k, b], cl[k, b] = high, low

    def surfaces(k):
        @pl.when(s > 0)
        def _():
            to_upper[k].wait_recv()

        @pl.when(s < NZ - 1)
        def _():
            to_lower[k].wait_recv()

        for t, block in ((0, low_block), (1, up_block)):
            real_high, real_low = split(block[0, k])
            imag_high, imag_low = split(block[1, k])

            def matrix(real, imag):
                return jnp.concatenate(
                    [jnp.concatenate([real, imag], axis=1), jnp.concatenate([-imag, real], axis=1)], axis=0
                )

            right_high, right_low = matrix(real_high, imag_high), matrix(real_low, imag_low)
            for b in range(2):

                def side(ref):
                    lanes = pl.ds(t * SURF, SURF)
                    return jnp.concatenate([ref[k, b, pl.ds(0, SURF), lanes], ref[k, b, pl.ds(SURF, SURF), lanes]], axis=1)

                high, low = split(dot3(side(ch), side(cl), right_high, right_low, False))
                for part in range(2):
                    there = (b, pl.ds(part * SURF, SURF), pl.ds(t * SURF, SURF))
                    wh[there] = high[:, part * SURF : (part + 1) * SURF]
                    wl[there] = low[:, part * SURF : (part + 1) * SURF]
        for b in range(2):
            quad = dot3(wh[b], wl[b], ch[k, b], cl[k, b], True)
            here = pl.ds(b * SURF, SURF)
            out_ref[0, k, here, :] = quad[:SURF, :SURF] + quad[SURF:, SURF:]
            out_ref[1, k, here, :] = quad[SURF:, :SURF] - quad[:SURF, SURF:]

    @pl.when(s == 0)
    def _():
        surfaces(0)
        surfaces(1)

    arrived(reduced, 7, y_sem.at[1])
    own = reduced[0]
    for j in range(1, NY):
        own = own + reduced[j]
    zout[0] = own

    def to_higher(part, d):
        return pltpu.make_async_remote_copy(
            src_ref=zout.at[part], dst_ref=zin.at[d - 1], send_sem=zs_sem.at[d - 1], recv_sem=zr_sem.at[d - 1],
            device_id=(e, s + d), device_id_type=MESH,
        )

    ahead = [to_higher(0, d) for d in range(1, REACH)]
    carries = [to_higher(1, d) for d in range(4, REACH + 1)]
    each_ahead(ahead, range(1, 5), lambda copy: copy.start())
    hear(down_sem, 2, (s >= HALF) & (s <= NZ - 6))
    each_ahead(damps, range(5, REACH), lambda copy: copy.start())
    each_ahead(ahead, range(5, REACH), lambda copy: copy.start())

    @pl.when(s > 0)
    def _():
        surfaces(0)
        surfaces(1)

    def from_slot(buffer, sem, k):
        return pltpu.make_async_copy(buffer.at[k], buffer.at[k], sem.at[k])

    before[...] = jnp.zeros_like(before)

    count = jnp.where(s < LATE, jnp.minimum(s, NEAR), s - HALF)

    @pl.when(s > NEAR)
    def _():
        from_slot(zin, zr_sem, count).wait()
        before[...] = zin[count]

    def decayed(value, rate):
        return value * jnp.concatenate([rate, rate], axis=1)

    def scan_step(k, carried):
        slot = count - 1 - k
        from_slot(zin, zr_sem, slot).wait()
        from_slot(damp_in, dr_sem, slot).wait()
        return decayed(carried, damp_in[slot]) + zin[slot]

    carried = lax.fori_loop(0, count, scan_step, before[...])
    zout[1] = decayed(carried, damp[...]) + own
    each_carry((4,), lambda copy: copy.start())
    hear(down_sem, 2, s == HALF - 1)
    each_carry(range(5, REACH + 1), lambda copy: copy.start())
    sigma = own + carried
    for part in range(2):
        sigma_ref[part] = sigma[:, part * ORB : (part + 1) * ORB]

    for k in range(2):
        sigma_real, sigma_imag = sigma[k : k + 1, :ORB], sigma[k : k + 1, ORB:]
        for b in range(2):
            here = pl.ds(b * SURF, SURF)
            green_real, green_imag = green[0, k, here, :], green[1, k, here, :]
            real_high, real_low = split(green_real * sigma_real - green_imag * sigma_imag)
            imag_high, imag_low = split(green_real * sigma_imag + green_imag * sigma_real)
            quad = dot3(
                jnp.concatenate([real_high, imag_high], axis=0), jnp.concatenate([real_low, imag_low], axis=0),
                gh[k, b], gl[k, b], True,
            )
            out_ref[0, k, here, :] += quad[:SURF, :SURF] + quad[SURF:, SURF:]
            out_ref[1, k, here, :] += quad[SURF:, :SURF] - quad[:SURF, SURF:]

    arrived(gathered, 7, xc_sem.at[0])
    arrived(partial, 7, y_sem.at[0])
    each_ahead(damps, range(1, REACH), lambda copy: copy.wait_send())
    each_ahead(ahead, range(1, REACH), lambda copy: copy.wait_send())
    each_carry(range(4, REACH + 1), lambda copy: copy.wait_send())

    for k in range(2):

        @pl.when(s < NZ - 1)
        def _(k=k):
            to_upper[k].wait_send()

        @pl.when(s > 0)
        def _(k=k):
            to_lower[k].wait_send()


def store(out_ref, sigma_ref, out_hbm, sigma_hbm, sem):
    copies = [
        pltpu.make_async_copy(out_ref, out_hbm, sem.at[0]),
        pltpu.make_async_copy(sigma_ref, sigma_hbm, sem.at[1]),
    ]
    for copy in copies:
        copy.start()
    for copy in copies:
        copy.wait()


def local(*args):
    vmem, smem, dma = pltpu.VMEM, pltpu.SMEM, pltpu.SemaphoreType.DMA
    shapes = (jax.ShapeDtypeStruct((2, 2, 2 * SURF, SURF), F32), jax.ShapeDtypeStruct((2, 2, ORB), F32))
    results = pl.pallas_call(
        kernel,
        out_shape=shapes,
        in_specs=[pl.BlockSpec(memory_space=pltpu.HBM)] * 9,
        out_specs=(pl.BlockSpec(memory_space=vmem), pl.BlockSpec(memory_space=vmem)),
        scratch_shapes=[
            vmem((2, 2, 2 * SURF, ORB), F32),
            vmem((2, 2, 2 * SURF, ORB), BF16),
            vmem((2, 2, 2 * SURF, ORB), BF16),
            vmem((2, 2, 2 * SURF, 2 * SURF), BF16),
            vmem((2, 2, 2 * SURF, 2 * SURF), BF16),
            vmem((2 * SURF, ORB), BF16),
            vmem((2 * SURF, ORB), BF16),
            vmem((2, 2 * SURF, 2 * SURF), BF16),
            vmem((2, 2 * SURF, 2 * SURF), BF16),
            vmem((1, 2, NB, ORB), jnp.int32),
            vmem((1, 2, NB, ORB), F32),
            vmem((1, ORB), F32),
            vmem((2, 2, ORB), F32),
            smem((MODES,), jnp.int32),
            smem((MODES,), F32),
            smem((MODES,), F32),
            vmem((8, 2, 2, ORB), F32),
            vmem((16, 2 * ORB), F32),
            vmem((NY, 2, 2 * ORB), F32),
            vmem((NY, 2, 2 * ORB), F32),
            vmem((2, 2, 2 * ORB), F32),
            vmem((REACH, 2, 2 * ORB), F32),
            vmem((REACH - 1, 1, ORB), F32),
            vmem((2, 2 * ORB), F32),
            vmem((2, 2, SURF, SURF), F32),
            vmem((2, 2, SURF, SURF), F32),
            dma((8,)),
            dma((2,)),
            dma((2,)),
            dma((REACH,)),
            dma((REACH,)),
            dma((REACH - 1,)),
            dma((REACH - 1,)),
            dma((2, 2)),
            dma((2, 2)),
            pltpu.SemaphoreType.REGULAR((3,)),
            pltpu.SemaphoreType.REGULAR((2,)),
            pltpu.SemaphoreType.REGULAR((2, 2)),
        ],
        compiler_params=pltpu.CompilerParams(
            collective_id=0, has_side_effects=True, vmem_limit_bytes=48 * 1024 * 1024
        ),
        cost_estimate=pl.CostEstimate(flops=5_000_000_000, bytes_accessed=4_000_000, transcendentals=0),
    )(*(pltpu.with_memory_space_constraint(arg, pltpu.HBM) for arg in args))
    return pl.pallas_call(
        store,
        out_shape=shapes,
        in_specs=[pl.BlockSpec(memory_space=vmem)] * 2,
        out_specs=[pl.BlockSpec(memory_space=pl.ANY)] * 2,
        scratch_shapes=[dma((2,))],
    )(*(pltpu.with_memory_space_constraint(result, vmem) for result in results))


def solution(mesh):
    placed = (
        P(None, "energy", "slab", None),
        P(None, "energy", "slab", None),
        P(None, "energy", "slab"),
        P("slab", None, None, None),
        P("slab", None, None, None),
        P("slab", None),
        P(),
        P(),
        P(),
    )
    return jax.shard_map(
        local,
        mesh=mesh,
        in_specs=placed,
        out_specs=(P(None, "energy", "slab", None), P(None, "energy", "slab")),
        check_vma=False,
    )
```

```python
import jax
import jax.numpy as jnp
from jax import lax
from jax.experimental import pallas as pl
from jax.experimental.pallas import tpu as pltpu
from jax.sharding import PartitionSpec as P

MESH = pl.DeviceIdType.MESH
F32 = jnp.float32
BF16 = jnp.bfloat16
NX, NY, NC, NZ = 4, 8, 2, 16
REACH = 8
NEAR = 3
LATE = NZ - 4
HALF = 8
ORB = 512
SURF = 128
NB = 8
MODES = 8


def split(value):
    high = value.astype(BF16)
    return high, (value - high.astype(F32)).astype(BF16)


def dot3(left_high, left_low, right_high, right_low, transposed):
    dims = (((1,), (1 if transposed else 0,)), ((), ()))

    def one(left, right):
        return lax.dot_general(left, right, dims, preferred_element_type=F32)

    rows = left_high.shape[0]
    both = one(jnp.concatenate([left_low, left_high], axis=0), right_high)
    return one(left_high, right_low) + both[:rows] + both[rows:]


def kernel(
    green_hbm, less_hbm, diag_hbm, near_hbm, hop_hbm, damp_hbm, offset_hbm, strength_hbm, bose_hbm,
    out_ref, sigma_ref,
    green, gh, gl, ch, cl, cph, cpl, wh, wl,
    near, hop, damp, diag, offset, strength, bose,
    gathered, stacked, partial, reduced, zout, zin, damp_in, before, low_block, up_block,
    local_sem, xc_sem, y_sem, zs_sem, zr_sem, ds_sem, dr_sem, halo_send, halo_recv, down_sem, up_sem, ring_sem,
):
    e, s = lax.axis_index("energy"), lax.axis_index("slab")
    x, y, c = e // (NY * NC), lax.rem(e // NC, NY), lax.rem(e, NC)

    def at(px, py, pc):
        return (px * NY + py) * NC + pc

    xc_peers = []
    for d in (4, 5, 2, 3, 6, 7, 1):
        px, pc = lax.rem(x + d // NC, NX), lax.rem(c + d % NC, NC)
        xc_peers.append((at(px, y, pc), s))
    y_peers = [(lax.rem(y + d, NY), (at(x, lax.rem(y + d, NY), c), s)) for d in range(1, NY)]

    barrier = pltpu.get_barrier_semaphore()

    def tell(device):
        pl.semaphore_signal(barrier, inc=1, device_id=device, device_id_type=MESH)

    pairs = [
        (diag_hbm, diag), (damp_hbm, damp), (offset_hbm, offset), (strength_hbm, strength), (bose_hbm, bose),
        (near_hbm, near), (hop_hbm, hop), (green_hbm, green),
    ]
    loads = [pltpu.make_async_copy(a, b, local_sem.at[k]) for k, (a, b) in enumerate(pairs)]
    loads[0].start()
    for device in xc_peers:
        tell(device)
    for d in (1, NY - 1):
        tell(y_peers[d - 1][1])

    @pl.when(s < NZ - 1)
    def _():
        tell((e, s + 1))

    @pl.when(s > 0)
    def _():
        tell((e, s - 1))

    loads[0].wait()
    mine = x * NC + c
    gathered[mine] = diag[...]
    pl.semaphore_wait(barrier, 9 + jnp.where(s > 0, 1, 0) + jnp.where(s < NZ - 1, 1, 0))

    for device in xc_peers:
        pltpu.make_async_remote_copy(
            src_ref=diag, dst_ref=gathered.at[mine], send_sem=xc_sem.at[0], recv_sem=xc_sem.at[1],
            device_id=device, device_id_type=MESH,
        ).start()

    to_upper = [
        pltpu.make_async_remote_copy(
            src_ref=less_hbm.at[:, k, pl.ds(SURF, SURF), :], dst_ref=low_block.at[:, k],
            send_sem=halo_send.at[0, k], recv_sem=halo_recv.at[0, k], device_id=(e, s + 1), device_id_type=MESH,
        )
        for k in range(2)
    ]
    to_lower = [
        pltpu.make_async_remote_copy(
            src_ref=less_hbm.at[:, k, pl.ds(0, SURF), :], dst_ref=up_block.at[:, k],
            send_sem=halo_send.at[1, k], recv_sem=halo_recv.at[1, k], device_id=(e, s - 1), device_id_type=MESH,
        )
        for k in range(2)
    ]
    for k in range(2):

        @pl.when(s < NZ - 1)
        def _(k=k):
            to_upper[k].start()

        @pl.when(s > 0)
        def _(k=k):
            to_lower[k].start()

    for load in loads[1:]:
        load.start()

    def pass_on(sem, step, when, there):
        @pl.when(when)
        def _():
            pl.semaphore_signal(sem.at[step], inc=1, device_id=(e, there), device_id_type=MESH)

    def hear(sem, step, when):
        @pl.when(when)
        def _():
            pl.semaphore_wait(sem.at[step], 1)

    def ring_round(step):
        for way, d in ((0, step), (1, NY - step)):
            pl.semaphore_signal(ring_sem.at[step - 1, way], inc=1, device_id=y_peers[d - 1][1], device_id_type=MESH)

    def ring_wait(step, *ways):
        for way in ways:
            pl.semaphore_wait(ring_sem.at[step - 1, way], 1)

    ring_round(1)
    pass_on(down_sem, 0, (s >= 1) & (s <= NZ - 2), s - 1)
    pass_on(up_sem, 0, (s >= 1) & (s <= NZ - 2), s + 1)

    @pl.when(s == 0)
    def _():
        low_block[...] = jnp.zeros_like(low_block)

    @pl.when(s == NZ - 1)
    def _():
        up_block[...] = jnp.zeros_like(up_block)

    for load in loads[1:5]:
        load.wait()
    rows = lax.broadcasted_iota(jnp.int32, (16, 16), 0)
    cols = lax.broadcasted_iota(jnp.int32, (16, 16), 1)
    energy_to = x * 32 + (rows // 2) * 4 + c * 2 + lax.rem(rows, 2)
    energy_from = (cols // 4) * 32 + y * 4 + lax.rem(cols, 4)
    gap = energy_from - energy_to
    coupling = jnp.zeros((16, 16), F32)
    for q in range(MODES):
        emitted = (gap == offset[q]).astype(F32)
        absorbed = (gap == -offset[q]).astype(F32)
        coupling = coupling + strength[q] * ((bose[q] + 1.0) * emitted + bose[q] * absorbed)

    loads[5].wait()
    loads[6].wait()
    slots = lax.broadcasted_iota(jnp.int32, (SURF, ORB), 0)
    for t in range(2):
        couple = jnp.zeros((SURF, ORB), F32)
        for k in range(NB):
            couple = couple + jnp.where(near[0, t, k : k + 1, :] == slots, hop[0, t, k : k + 1, :], 0.0)
        cph[pl.ds(t * SURF, SURF)], cpl[pl.ds(t * SURF, SURF)] = split(couple)
    loads[7].wait()
    for k in range(2):
        for b in range(2):
            for part in range(2):
                high, low = split(green[part, k, pl.ds(b * SURF, SURF), :])
                gh[k, b, pl.ds(part * SURF, SURF), :] = high
                gl[k, b, pl.ds(part * SURF, SURF), :] = low

    ring_wait(1, 0, 1)
    ring_round(2)
    hear(down_sem, 0, s <= NZ - 3)
    hear(up_sem, 0, s >= 2)
    pass_on(down_sem, 1, (s >= 2) & (s <= NZ - 2), s - 2)
    pass_on(up_sem, 1, (s >= LATE - 3) & (s <= NZ - 4), s + 2)

    def arrived(buffer, count, sem):
        pltpu.make_async_copy(buffer.at[pl.ds(0, count)], buffer.at[pl.ds(0, count)], sem).wait()

    arrived(gathered, 7, xc_sem.at[1])
    for j in range(8):
        for part in range(2):
            stacked[pl.ds(2 * j, 2), pl.ds(part * ORB, ORB)] = gathered[j, part]
    product = jnp.dot(coupling, stacked[...], precision=lax.Precision.HIGHEST, preferred_element_type=F32)
    for j in range(NY):
        partial[j] = product[2 * j : 2 * j + 2, :]
    for d in (2, 6, 1, 7, 4, 5, 3):
        if d == 4:
            ring_wait(2, 0)
        if d == 3:
            ring_wait(2, 1)
        there, device = y_peers[d - 1]
        pltpu.make_async_remote_copy(
            src_ref=partial.at[there], dst_ref=reduced.at[y], send_sem=y_sem.at[0], recv_sem=y_sem.at[1],
            device_id=device, device_id_type=MESH,
        ).start()
    reduced[y] = partial[y]

    hear(down_sem, 1, s <= NZ - 4)
    hear(up_sem, 1, (s >= LATE - 1) & (s <= NZ - 2))
    pass_on(down_sem, 2, (s >= LATE - 1) & (s <= NZ - 2), s - 4)
    damps = [
        pltpu.make_async_remote_copy(
            src_ref=damp, dst_ref=damp_in.at[d - 1], send_sem=ds_sem.at[d - 1], recv_sem=dr_sem.at[d - 1],
            device_id=(e, s + d), device_id_type=MESH,
        )
        for d in range(1, REACH)
    ]

    def each_ahead(copies, distances, act):
        for d in distances:

            @pl.when((s + d < NZ) & ((d <= NEAR) | (s >= HALF)))
            def _(d=d):
                act(copies[d - 1])

    def each_carry(distances, act):
        for d in distances:

            @pl.when((s == HALF - 1) | ((d == 4) & (s < HALF)))
            def _(d=d):
                act(carries[d - 4])

    each_ahead(damps, range(1, 5), lambda copy: copy.start())

    for k in range(2):
        for b in range(2):
            high, low = split(dot3(gh[k, b], gl[k, b], cph[...], cpl[...], True))
            ch[k, b], cl[k, b] = high, low

    def surfaces(k):
        @pl.when(s > 0)
        def _():
            to_upper[k].wait_recv()

        @pl.when(s < NZ - 1)
        def _():
            to_lower[k].wait_recv()

        for t, block in ((0, low_block), (1, up_block)):
            real_high, real_low = split(block[0, k])
            imag_high, imag_low = split(block[1, k])

            def matrix(real, imag):
                return jnp.concatenate(
                    [jnp.concatenate([real, imag], axis=1), jnp.concatenate([-imag, real], axis=1)], axis=0
                )

            right_high, right_low = matrix(real_high, imag_high), matrix(real_low, imag_low)
            for b in range(2):

                def side(ref):
                    lanes = pl.ds(t * SURF, SURF)
                    return jnp.concatenate([ref[k, b, pl.ds(0, SURF), lanes], ref[k, b, pl.ds(SURF, SURF), lanes]], axis=1)

                high, low = split(dot3(side(ch), side(cl), right_high, right_low, False))
                for part in range(2):
                    there = (b, pl.ds(part * SURF, SURF), pl.ds(t * SURF, SURF))
                    wh[there] = high[:, part * SURF : (part + 1) * SURF]
                    wl[there] = low[:, part * SURF : (part + 1) * SURF]
        for b in range(2):
            quad = dot3(wh[b], wl[b], ch[k, b], cl[k, b], True)
            here = pl.ds(b * SURF, SURF)
            out_ref[0, k, here, :] = quad[:SURF, :SURF] + quad[SURF:, SURF:]
            out_ref[1, k, here, :] = quad[SURF:, :SURF] - quad[:SURF, SURF:]

    early = (s == 0) & (e > 0)

    @pl.when(early)
    def _():
        surfaces(0)
        surfaces(1)

    arrived(reduced, 7, y_sem.at[1])
    own = reduced[0]
    for j in range(1, NY):
        own = own + reduced[j]
    zout[0] = own

    def to_higher(part, d):
        return pltpu.make_async_remote_copy(
            src_ref=zout.at[part], dst_ref=zin.at[d - 1], send_sem=zs_sem.at[d - 1], recv_sem=zr_sem.at[d - 1],
            device_id=(e, s + d), device_id_type=MESH,
        )

    ahead = [to_higher(0, d) for d in range(1, REACH)]
    carries = [to_higher(1, d) for d in range(4, REACH + 1)]
    each_ahead(ahead, range(1, 5), lambda copy: copy.start())
    hear(down_sem, 2, (s >= HALF) & (s <= NZ - 6))
    each_ahead(damps, range(5, REACH), lambda copy: copy.start())
    each_ahead(ahead, range(5, REACH), lambda copy: copy.start())

    @pl.when(jnp.logical_not(early))
    def _():
        surfaces(0)
        surfaces(1)

    def from_slot(buffer, sem, k):
        return pltpu.make_async_copy(buffer.at[k], buffer.at[k], sem.at[k])

    before[...] = jnp.zeros_like(before)

    count = jnp.where(s < LATE, jnp.minimum(s, NEAR), s - HALF)

    @pl.when(s > NEAR)
    def _():
        from_slot(zin, zr_sem, count).wait()
        before[...] = zin[count]

    def decayed(value, rate):
        return value * jnp.concatenate([rate, rate], axis=1)

    def scan_step(k, carried):
        slot = count - 1 - k
        from_slot(zin, zr_sem, slot).wait()
        from_slot(damp_in, dr_sem, slot).wait()
        return decayed(carried, damp_in[slot]) + zin[slot]

    carried = lax.fori_loop(0, count, scan_step, before[...])
    zout[1] = decayed(carried, damp[...]) + own
    each_carry((4,), lambda copy: copy.start())
    hear(down_sem, 2, s == HALF - 1)
    each_carry(range(5, REACH + 1), lambda copy: copy.start())
    sigma = own + carried
    for part in range(2):
        sigma_ref[part] = sigma[:, part * ORB : (part + 1) * ORB]

    for k in range(2):
        sigma_real, sigma_imag = sigma[k : k + 1, :ORB], sigma[k : k + 1, ORB:]
        for b in range(2):
            here = pl.ds(b * SURF, SURF)
            green_real, green_imag = green[0, k, here, :], green[1, k, here, :]
            real_high, real_low = split(green_real * sigma_real - green_imag * sigma_imag)
            imag_high, imag_low = split(green_real * sigma_imag + green_imag * sigma_real)
            quad = dot3(
                jnp.concatenate([real_high, imag_high], axis=0), jnp.concatenate([real_low, imag_low], axis=0),
                gh[k, b], gl[k, b], True,
            )
            out_ref[0, k, here, :] += quad[:SURF, :SURF] + quad[SURF:, SURF:]
            out_ref[1, k, here, :] += quad[SURF:, :SURF] - quad[:SURF, SURF:]

    arrived(gathered, 7, xc_sem.at[0])
    arrived(partial, 7, y_sem.at[0])
    each_ahead(damps, range(1, REACH), lambda copy: copy.wait_send())
    each_ahead(ahead, range(1, REACH), lambda copy: copy.wait_send())
    each_carry(range(4, REACH + 1), lambda copy: copy.wait_send())

    for k in range(2):

        @pl.when(s < NZ - 1)
        def _(k=k):
            to_upper[k].wait_send()

        @pl.when(s > 0)
        def _(k=k):
            to_lower[k].wait_send()


def store(out_ref, sigma_ref, out_hbm, sigma_hbm, sem):
    copies = [pltpu.make_async_copy(sigma_ref, sigma_hbm, sem.at[0])]
    for part in range(2):
        for k in range(2):
            for b in range(2):
                here = (part, k, pl.ds(b * SURF, SURF))
                copies.append(pltpu.make_async_copy(out_ref.at[here], out_hbm.at[here], sem.at[len(copies)]))
    for copy in copies:
        copy.start()
    for copy in copies:
        copy.wait()


def local(*args):
    vmem, smem, dma = pltpu.VMEM, pltpu.SMEM, pltpu.SemaphoreType.DMA
    shapes = (jax.ShapeDtypeStruct((2, 2, 2 * SURF, SURF), F32), jax.ShapeDtypeStruct((2, 2, ORB), F32))
    results = pl.pallas_call(
        kernel,
        out_shape=shapes,
        in_specs=[pl.BlockSpec(memory_space=pltpu.HBM)] * 9,
        out_specs=(pl.BlockSpec(memory_space=vmem), pl.BlockSpec(memory_space=vmem)),
        scratch_shapes=[
            vmem((2, 2, 2 * SURF, ORB), F32),
            vmem((2, 2, 2 * SURF, ORB), BF16),
            vmem((2, 2, 2 * SURF, ORB), BF16),
            vmem((2, 2, 2 * SURF, 2 * SURF), BF16),
            vmem((2, 2, 2 * SURF, 2 * SURF), BF16),
            vmem((2 * SURF, ORB), BF16),
            vmem((2 * SURF, ORB), BF16),
            vmem((2, 2 * SURF, 2 * SURF), BF16),
            vmem((2, 2 * SURF, 2 * SURF), BF16),
            vmem((1, 2, NB, ORB), jnp.int32),
            vmem((1, 2, NB, ORB), F32),
            vmem((1, ORB), F32),
            vmem((2, 2, ORB), F32),
            smem((MODES,), jnp.int32),
            smem((MODES,), F32),
            smem((MODES,), F32),
            vmem((8, 2, 2, ORB), F32),
            vmem((16, 2 * ORB), F32),
            vmem((NY, 2, 2 * ORB), F32),
            vmem((NY, 2, 2 * ORB), F32),
            vmem((2, 2, 2 * ORB), F32),
            vmem((REACH, 2, 2 * ORB), F32),
            vmem((REACH - 1, 1, ORB), F32),
            vmem((2, 2 * ORB), F32),
            vmem((2, 2, SURF, SURF), F32),
            vmem((2, 2, SURF, SURF), F32),
            dma((8,)),
            dma((2,)),
            dma((2,)),
            dma((REACH,)),
            dma((REACH,)),
            dma((REACH - 1,)),
            dma((REACH - 1,)),
            dma((2, 2)),
            dma((2, 2)),
            pltpu.SemaphoreType.REGULAR((3,)),
            pltpu.SemaphoreType.REGULAR((2,)),
            pltpu.SemaphoreType.REGULAR((2, 2)),
        ],
        compiler_params=pltpu.CompilerParams(
            collective_id=0, has_side_effects=True, vmem_limit_bytes=48 * 1024 * 1024
        ),
        cost_estimate=pl.CostEstimate(flops=5_000_000_000, bytes_accessed=4_000_000, transcendentals=0),
    )(*(pltpu.with_memory_space_constraint(arg, pltpu.HBM) for arg in args))
    return pl.pallas_call(
        store,
        out_shape=shapes,
        in_specs=[pl.BlockSpec(memory_space=vmem)] * 2,
        out_specs=[pl.BlockSpec(memory_space=pl.ANY)] * 2,
        scratch_shapes=[dma((9,))],
    )(*(pltpu.with_memory_space_constraint(result, vmem) for result in results))


def solution(mesh):
    placed = (
        P(None, "energy", "slab", None),
        P(None, "energy", "slab", None),
        P(None, "energy", "slab"),
        P("slab", None, None, None),
        P("slab", None, None, None),
        P("slab", None),
        P(),
        P(),
        P(),
    )
    return jax.shard_map(
        local,
        mesh=mesh,
        in_specs=placed,
        out_specs=(P(None, "energy", "slab", None), P(None, "energy", "slab")),
        check_vma=False,
    )
```

```python
import jax
import jax.numpy as jnp
from jax import lax
from jax.experimental import pallas as pl
from jax.experimental.pallas import tpu as pltpu
from jax.sharding import PartitionSpec as P

MESH = pl.DeviceIdType.MESH
F32 = jnp.float32
BF16 = jnp.bfloat16
NX, NY, NC, NZ = 4, 8, 2, 16
REACH = 8
NEAR = 3
LATE = NZ - 4
HALF = 8
ORB = 512
SURF = 128
NB = 8
MODES = 8


def split(value):
    high = value.astype(BF16)
    return high, (value - high.astype(F32)).astype(BF16)


def dot3(left_high, left_low, right_high, right_low, transposed):
    dims = (((1,), (1 if transposed else 0,)), ((), ()))

    def one(left, right):
        return lax.dot_general(left, right, dims, preferred_element_type=F32)

    rows = left_high.shape[0]
    both = one(jnp.concatenate([left_low, left_high], axis=0), right_high)
    return one(left_high, right_low) + both[:rows] + both[rows:]


def kernel(
    green_hbm, less_hbm, diag_hbm, near_hbm, hop_hbm, damp_hbm, offset_hbm, strength_hbm, bose_hbm,
    out_ref, sigma_ref,
    green, gh, gl, ch, cl, cph, cpl, wh, wl,
    near, hop, damp, diag, offset, strength, bose,
    gathered, stacked, partial, reduced, zout, zin, damp_in, before, low_block, up_block,
    local_sem, xc_sem, y_sem, zs_sem, zr_sem, ds_sem, dr_sem, halo_send, halo_recv, down_sem, up_sem, ring_sem,
):
    e, s = lax.axis_index("energy"), lax.axis_index("slab")
    x, y, c = e // (NY * NC), lax.rem(e // NC, NY), lax.rem(e, NC)

    def at(px, py, pc):
        return (px * NY + py) * NC + pc

    xc_peers = []
    for d in (4, 5, 2, 3, 6, 7, 1):
        px, pc = lax.rem(x + d // NC, NX), lax.rem(c + d % NC, NC)
        xc_peers.append((at(px, y, pc), s))
    y_peers = [(lax.rem(y + d, NY), (at(x, lax.rem(y + d, NY), c), s)) for d in range(1, NY)]

    barrier = pltpu.get_barrier_semaphore()

    def tell(device):
        pl.semaphore_signal(barrier, inc=1, device_id=device, device_id_type=MESH)

    pairs = [
        (diag_hbm, diag), (damp_hbm, damp), (offset_hbm, offset), (strength_hbm, strength), (bose_hbm, bose),
        (near_hbm, near), (hop_hbm, hop), (green_hbm, green),
    ]
    loads = [pltpu.make_async_copy(a, b, local_sem.at[k]) for k, (a, b) in enumerate(pairs)]
    loads[0].start()
    for d in (1, NY - 1):
        tell(y_peers[d - 1][1])

    @pl.when(s < NZ - 1)
    def _():
        tell((e, s + 1))

    @pl.when(s > 0)
    def _():
        tell((e, s - 1))

    for device in xc_peers:
        tell(device)

    loads[0].wait()
    mine = x * NC + c
    gathered[mine] = diag[...]
    pl.semaphore_wait(barrier, 9 + jnp.where(s > 0, 1, 0) + jnp.where(s < NZ - 1, 1, 0))

    for device in xc_peers:
        pltpu.make_async_remote_copy(
            src_ref=diag, dst_ref=gathered.at[mine], send_sem=xc_sem.at[0], recv_sem=xc_sem.at[1],
            device_id=device, device_id_type=MESH,
        ).start()

    to_upper = [
        pltpu.make_async_remote_copy(
            src_ref=less_hbm.at[:, k, pl.ds(SURF, SURF), :], dst_ref=low_block.at[:, k],
            send_sem=halo_send.at[0, k], recv_sem=halo_recv.at[0, k], device_id=(e, s + 1), device_id_type=MESH,
        )
        for k in range(2)
    ]
    to_lower = [
        pltpu.make_async_remote_copy(
            src_ref=less_hbm.at[:, k, pl.ds(0, SURF), :], dst_ref=up_block.at[:, k],
            send_sem=halo_send.at[1, k], recv_sem=halo_recv.at[1, k], device_id=(e, s - 1), device_id_type=MESH,
        )
        for k in range(2)
    ]
    for k in range(2):

        @pl.when(s < NZ - 1)
        def _(k=k):
            to_upper[k].start()

        @pl.when(s > 0)
        def _(k=k):
            to_lower[k].start()

    for load in loads[1:]:
        load.start()

    def pass_on(sem, step, when, there):
        @pl.when(when)
        def _():
            pl.semaphore_signal(sem.at[step], inc=1, device_id=(e, there), device_id_type=MESH)

    def hear(sem, step, when):
        @pl.when(when)
        def _():
            pl.semaphore_wait(sem.at[step], 1)

    def ring_round(step):
        for way, d in ((0, step), (1, NY - step)):
            pl.semaphore_signal(ring_sem.at[step - 1, way], inc=1, device_id=y_peers[d - 1][1], device_id_type=MESH)

    def ring_wait(step, *ways):
        for way in ways:
            pl.semaphore_wait(ring_sem.at[step - 1, way], 1)

    ring_round(1)
    pass_on(down_sem, 0, (s >= 1) & (s <= NZ - 2), s - 1)
    pass_on(up_sem, 0, (s >= 1) & (s <= NZ - 2), s + 1)

    @pl.when(s == 0)
    def _():
        low_block[...] = jnp.zeros_like(low_block)

    @pl.when(s == NZ - 1)
    def _():
        up_block[...] = jnp.zeros_like(up_block)

    for load in loads[1:5]:
        load.wait()
    rows = lax.broadcasted_iota(jnp.int32, (16, 16), 0)
    cols = lax.broadcasted_iota(jnp.int32, (16, 16), 1)
    energy_to = x * 32 + (rows // 2) * 4 + c * 2 + lax.rem(rows, 2)
    energy_from = (cols // 4) * 32 + y * 4 + lax.rem(cols, 4)
    gap = energy_from - energy_to
    coupling = jnp.zeros((16, 16), F32)
    for q in range(MODES):
        emitted = (gap == offset[q]).astype(F32)
        absorbed = (gap == -offset[q]).astype(F32)
        coupling = coupling + strength[q] * ((bose[q] + 1.0) * emitted + bose[q] * absorbed)

    loads[5].wait()
    loads[6].wait()
    slots = lax.broadcasted_iota(jnp.int32, (SURF, ORB), 0)
    for t in range(2):
        couple = jnp.zeros((SURF, ORB), F32)
        for k in range(NB):
            couple = couple + jnp.where(near[0, t, k : k + 1, :] == slots, hop[0, t, k : k + 1, :], 0.0)
        cph[pl.ds(t * SURF, SURF)], cpl[pl.ds(t * SURF, SURF)] = split(couple)
    loads[7].wait()
    for k in range(2):
        for b in range(2):
            for part in range(2):
                high, low = split(green[part, k, pl.ds(b * SURF, SURF), :])
                gh[k, b, pl.ds(part * SURF, SURF), :] = high
                gl[k, b, pl.ds(part * SURF, SURF), :] = low

    ring_wait(1, 0, 1)
    ring_round(2)
    hear(down_sem, 0, s <= NZ - 3)
    hear(up_sem, 0, s >= 2)
    pass_on(down_sem, 1, (s >= 2) & (s <= NZ - 2), s - 2)
    pass_on(up_sem, 1, (s >= LATE - 3) & (s <= NZ - 4), s + 2)

    def arrived(buffer, count, sem):
        pltpu.make_async_copy(buffer.at[pl.ds(0, count)], buffer.at[pl.ds(0, count)], sem).wait()

    arrived(gathered, 7, xc_sem.at[1])
    for j in range(8):
        for part in range(2):
            stacked[pl.ds(2 * j, 2), pl.ds(part * ORB, ORB)] = gathered[j, part]
    product = jnp.dot(coupling, stacked[...], precision=lax.Precision.HIGHEST, preferred_element_type=F32)
    for j in range(NY):
        partial[j] = product[2 * j : 2 * j + 2, :]
    for d in (2, 6, 1, 7, 4, 5, 3):
        if d == 4:
            ring_wait(2, 0)
        if d == 3:
            ring_wait(2, 1)
        there, device = y_peers[d - 1]
        pltpu.make_async_remote_copy(
            src_ref=partial.at[there], dst_ref=reduced.at[y], send_sem=y_sem.at[0], recv_sem=y_sem.at[1],
            device_id=device, device_id_type=MESH,
        ).start()
    reduced[y] = partial[y]

    hear(down_sem, 1, s <= NZ - 4)
    hear(up_sem, 1, (s >= LATE - 1) & (s <= NZ - 2))
    pass_on(down_sem, 2, (s >= LATE - 1) & (s <= NZ - 2), s - 4)
    damps = [
        pltpu.make_async_remote_copy(
            src_ref=damp, dst_ref=damp_in.at[d - 1], send_sem=ds_sem.at[d - 1], recv_sem=dr_sem.at[d - 1],
            device_id=(e, s + d), device_id_type=MESH,
        )
        for d in range(1, REACH)
    ]

    def each_ahead(copies, distances, act):
        for d in distances:

            @pl.when((s + d < NZ) & ((d <= NEAR) | (s >= HALF)))
            def _(d=d):
                act(copies[d - 1])

    def each_carry(distances, act):
        for d in distances:

            @pl.when((s == HALF - 1) | ((d == 4) & (s < HALF)))
            def _(d=d):
                act(carries[d - 4])

    each_ahead(damps, range(1, 5), lambda copy: copy.start())

    for k in range(2):
        for b in range(2):
            high, low = split(dot3(gh[k, b], gl[k, b], cph[...], cpl[...], True))
            ch[k, b], cl[k, b] = high, low

    def surfaces(k):
        @pl.when(s > 0)
        def _():
            to_upper[k].wait_recv()

        @pl.when(s < NZ - 1)
        def _():
            to_lower[k].wait_recv()

        for t, block in ((0, low_block), (1, up_block)):
            real_high, real_low = split(block[0, k])
            imag_high, imag_low = split(block[1, k])

            def matrix(real, imag):
                return jnp.concatenate(
                    [jnp.concatenate([real, imag], axis=1), jnp.concatenate([-imag, real], axis=1)], axis=0
                )

            right_high, right_low = matrix(real_high, imag_high), matrix(real_low, imag_low)
            for b in range(2):

                def side(ref):
                    lanes = pl.ds(t * SURF, SURF)
                    return jnp.concatenate([ref[k, b, pl.ds(0, SURF), lanes], ref[k, b, pl.ds(SURF, SURF), lanes]], axis=1)

                high, low = split(dot3(side(ch), side(cl), right_high, right_low, False))
                for part in range(2):
                    there = (b, pl.ds(part * SURF, SURF), pl.ds(t * SURF, SURF))
                    wh[there] = high[:, part * SURF : (part + 1) * SURF]
                    wl[there] = low[:, part * SURF : (part + 1) * SURF]
        for b in range(2):
            quad = dot3(wh[b], wl[b], ch[k, b], cl[k, b], True)
            here = pl.ds(b * SURF, SURF)
            out_ref[0, k, here, :] = quad[:SURF, :SURF] + quad[SURF:, SURF:]
            out_ref[1, k, here, :] = quad[SURF:, :SURF] - quad[:SURF, SURF:]

    early = (s == 0) & (e > 0)

    @pl.when(early)
    def _():
        surfaces(0)
        surfaces(1)

    arrived(reduced, 7, y_sem.at[1])
    own = reduced[0]
    for j in range(1, NY):
        own = own + reduced[j]
    zout[0] = own

    def to_higher(part, d):
        return pltpu.make_async_remote_copy(
            src_ref=zout.at[part], dst_ref=zin.at[d - 1], send_sem=zs_sem.at[d - 1], recv_sem=zr_sem.at[d - 1],
            device_id=(e, s + d), device_id_type=MESH,
        )

    ahead = [to_higher(0, d) for d in range(1, REACH)]
    carries = [to_higher(1, d) for d in range(4, REACH + 1)]
    each_ahead(ahead, range(1, 5), lambda copy: copy.start())
    hear(down_sem, 2, (s >= HALF) & (s <= NZ - 6))
    each_ahead(damps, range(5, REACH), lambda copy: copy.start())
    each_ahead(ahead, range(5, REACH), lambda copy: copy.start())

    @pl.when(jnp.logical_not(early))
    def _():
        surfaces(0)
        surfaces(1)

    def from_slot(buffer, sem, k):
        return pltpu.make_async_copy(buffer.at[k], buffer.at[k], sem.at[k])

    before[...] = jnp.zeros_like(before)

    count = jnp.where(s < LATE, jnp.minimum(s, NEAR), s - HALF)

    @pl.when(s > NEAR)
    def _():
        from_slot(zin, zr_sem, count).wait()
        before[...] = zin[count]

    def decayed(value, rate):
        return value * jnp.concatenate([rate, rate], axis=1)

    def scan_step(k, carried):
        slot = count - 1 - k
        from_slot(zin, zr_sem, slot).wait()
        from_slot(damp_in, dr_sem, slot).wait()
        return decayed(carried, damp_in[slot]) + zin[slot]

    carried = lax.fori_loop(0, count, scan_step, before[...])
    zout[1] = decayed(carried, damp[...]) + own
    each_carry((4,), lambda copy: copy.start())
    hear(down_sem, 2, s == HALF - 1)
    each_carry(range(5, REACH + 1), lambda copy: copy.start())
    sigma = own + carried
    for part in range(2):
        sigma_ref[part] = sigma[:, part * ORB : (part + 1) * ORB]

    for k in range(2):
        sigma_real, sigma_imag = sigma[k : k + 1, :ORB], sigma[k : k + 1, ORB:]
        for b in range(2):
            here = pl.ds(b * SURF, SURF)
            green_real, green_imag = green[0, k, here, :], green[1, k, here, :]
            real_high, real_low = split(green_real * sigma_real - green_imag * sigma_imag)
            imag_high, imag_low = split(green_real * sigma_imag + green_imag * sigma_real)
            quad = dot3(
                jnp.concatenate([real_high, imag_high], axis=0), jnp.concatenate([real_low, imag_low], axis=0),
                gh[k, b], gl[k, b], True,
            )
            out_ref[0, k, here, :] += quad[:SURF, :SURF] + quad[SURF:, SURF:]
            out_ref[1, k, here, :] += quad[SURF:, :SURF] - quad[:SURF, SURF:]

    arrived(gathered, 7, xc_sem.at[0])
    arrived(partial, 7, y_sem.at[0])
    each_ahead(damps, range(1, REACH), lambda copy: copy.wait_send())
    each_ahead(ahead, range(1, REACH), lambda copy: copy.wait_send())
    each_carry(range(4, REACH + 1), lambda copy: copy.wait_send())

    for k in range(2):

        @pl.when(s < NZ - 1)
        def _(k=k):
            to_upper[k].wait_send()

        @pl.when(s > 0)
        def _(k=k):
            to_lower[k].wait_send()


def store(out_ref, sigma_ref, out_hbm, sigma_hbm, sem):
    copies = [pltpu.make_async_copy(sigma_ref, sigma_hbm, sem.at[0])]
    for part in range(2):
        for k in range(2):
            for b in range(2):
                here = (part, k, pl.ds(b * SURF, SURF))
                copies.append(pltpu.make_async_copy(out_ref.at[here], out_hbm.at[here], sem.at[len(copies)]))
    for copy in copies:
        copy.start()
    for copy in copies:
        copy.wait()


def local(*args):
    vmem, smem, dma = pltpu.VMEM, pltpu.SMEM, pltpu.SemaphoreType.DMA
    shapes = (jax.ShapeDtypeStruct((2, 2, 2 * SURF, SURF), F32), jax.ShapeDtypeStruct((2, 2, ORB), F32))
    results = pl.pallas_call(
        kernel,
        out_shape=shapes,
        in_specs=[pl.BlockSpec(memory_space=pltpu.HBM)] * 9,
        out_specs=(pl.BlockSpec(memory_space=vmem), pl.BlockSpec(memory_space=vmem)),
        scratch_shapes=[
            vmem((2, 2, 2 * SURF, ORB), F32),
            vmem((2, 2, 2 * SURF, ORB), BF16),
            vmem((2, 2, 2 * SURF, ORB), BF16),
            vmem((2, 2, 2 * SURF, 2 * SURF), BF16),
            vmem((2, 2, 2 * SURF, 2 * SURF), BF16),
            vmem((2 * SURF, ORB), BF16),
            vmem((2 * SURF, ORB), BF16),
            vmem((2, 2 * SURF, 2 * SURF), BF16),
            vmem((2, 2 * SURF, 2 * SURF), BF16),
            vmem((1, 2, NB, ORB), jnp.int32),
            vmem((1, 2, NB, ORB), F32),
            vmem((1, ORB), F32),
            vmem((2, 2, ORB), F32),
            smem((MODES,), jnp.int32),
            smem((MODES,), F32),
            smem((MODES,), F32),
            vmem((8, 2, 2, ORB), F32),
            vmem((16, 2 * ORB), F32),
            vmem((NY, 2, 2 * ORB), F32),
            vmem((NY, 2, 2 * ORB), F32),
            vmem((2, 2, 2 * ORB), F32),
            vmem((REACH, 2, 2 * ORB), F32),
            vmem((REACH - 1, 1, ORB), F32),
            vmem((2, 2 * ORB), F32),
            vmem((2, 2, SURF, SURF), F32),
            vmem((2, 2, SURF, SURF), F32),
            dma((8,)),
            dma((2,)),
            dma((2,)),
            dma((REACH,)),
            dma((REACH,)),
            dma((REACH - 1,)),
            dma((REACH - 1,)),
            dma((2, 2)),
            dma((2, 2)),
            pltpu.SemaphoreType.REGULAR((3,)),
            pltpu.SemaphoreType.REGULAR((2,)),
            pltpu.SemaphoreType.REGULAR((2, 2)),
        ],
        compiler_params=pltpu.CompilerParams(
            collective_id=0, has_side_effects=True, vmem_limit_bytes=48 * 1024 * 1024
        ),
        cost_estimate=pl.CostEstimate(flops=5_000_000_000, bytes_accessed=4_000_000, transcendentals=0),
    )(*(pltpu.with_memory_space_constraint(arg, pltpu.HBM) for arg in args))
    return pl.pallas_call(
        store,
        out_shape=shapes,
        in_specs=[pl.BlockSpec(memory_space=vmem)] * 2,
        out_specs=[pl.BlockSpec(memory_space=pl.ANY)] * 2,
        scratch_shapes=[dma((9,))],
    )(*(pltpu.with_memory_space_constraint(result, vmem) for result in results))


def solution(mesh):
    placed = (
        P(None, "energy", "slab", None),
        P(None, "energy", "slab", None),
        P(None, "energy", "slab"),
        P("slab", None, None, None),
        P("slab", None, None, None),
        P("slab", None),
        P(),
        P(),
        P(),
    )
    return jax.shard_map(
        local,
        mesh=mesh,
        in_specs=placed,
        out_specs=(P(None, "energy", "slab", None), P(None, "energy", "slab")),
        check_vma=False,
    )
```
